32 devices in a mesh: dp: 8 (over z, y), tensor: 4 (over x, core).
Axes of the slice: x: 2, y: 2, z: 4, core: 2. Of those that a mesh axis runs over, the one named last changes fastest.
Arguments:
- decoder_input: bfloat16 [8, 1024, 768], P('dp'), may hold values from -6 to 6
- encoder_states: bfloat16 [8, 2048, 768], P('dp'), may hold values from -6 to 6
- span_counts: int32 [8], P('dp'), may hold values from 1 to 4, as said below
- retrieved: int32 [8, 1024, 256], P('dp'), may hold values from 0 to 2047, as said below
- self_query: bfloat16 [768, 768], P(None, 'tensor'), may hold values from -0.21875 to 0.21875
- self_query_bias: bfloat16 [768], P('tensor'), may hold values from -3 to 3
- self_key: bfloat16 [768, 768], P(None, 'tensor'), may hold values from -0.21875 to 0.21875
- self_value: bfloat16 [768, 768], P(None, 'tensor'), may hold values from -0.21875 to 0.21875
- self_value_bias: bfloat16 [768], P('tensor'), may hold values from -3 to 3
- self_output: bfloat16 [768, 768], P('tensor'), may hold values from -3.5 to 3.5
- self_output_bias: bfloat16 [768], replicated, may hold values from -2 to 2
- first_gain: bfloat16 [768], replicated, may hold values from 0.5 to 1.5
- first_shift: bfloat16 [768], replicated, may hold values from -2 to 2
- cross_query: bfloat16 [768, 768], P(None, 'tensor'), may hold values from -0.21875 to 0.21875
- cross_query_bias: bfloat16 [768], P('tensor'), may hold values from -3 to 3
- cross_key: bfloat16 [768, 768], P(None, 'tensor'), may hold values from -0.21875 to 0.21875
- cross_value: bfloat16 [768, 768], P(None, 'tensor'), may hold values from -0.21875 to 0.21875
- cross_value_bias: bfloat16 [768], P('tensor'), may hold values from -3 to 3
- cross_output: bfloat16 [768, 768], P('tensor'), may hold values from -3.5 to 3.5
- cross_output_bias: bfloat16 [768], replicated, may hold values from -2 to 2
- second_gain: bfloat16 [768], replicated, may hold values from 0.5 to 1.5
- second_shift: bfloat16 [768], replicated, may hold values from -2 to 2
- hidden_weight: bfloat16 [768, 3072], P(None, 'tensor'), may hold values from -0.21875 to 0.21875
- hidden_bias: bfloat16 [3072], P('tensor'), may hold values from -2 to 2
- return_weight: bfloat16 [3072, 768], P('tensor'), may hold values from -0.109375 to 0.109375
- return_bias: bfloat16 [768], replicated, may hold values from -2 to 2
- third_gain: bfloat16 [768], replicated, may hold values from 0.5 to 1.5
- third_shift: bfloat16 [768], replicated, may hold values from -2 to 2
- cotangent: bfloat16 [8, 1024, 768], P('dp'), may hold values from -6 to 6
Outputs:
- layer_output: bfloat16 [8, 1024, 768], P('dp')
- input_delta: bfloat16 [8, 1024, 768], P('dp')
- delta_self_query: float32 [768, 768], P(None, 'tensor')
- delta_self_query_bias: float32 [768], P('tensor')
- delta_self_key: float32 [768, 768], P(None, 'tensor')
- delta_self_value: float32 [768, 768], P(None, 'tensor')
- delta_self_value_bias: float32 [768], P('tensor')
- delta_self_output: float32 [768, 768], P('tensor')
- delta_self_output_bias: float32 [768], replicated
- delta_first_gain: float32 [768], replicated
- delta_first_shift: float32 [768], replicated
- delta_cross_query: float32 [768, 768], P(None, 'tensor')
- delta_cross_query_bias: float32 [768], P('tensor')
- delta_cross_key: float32 [768, 768], P(None, 'tensor')
- delta_cross_value: float32 [768, 768], P(None, 'tensor')
- delta_cross_value_bias: float32 [768], P('tensor')
- delta_cross_output: float32 [768, 768], P('tensor')
- delta_cross_output_bias: float32 [768], replicated
- delta_second_gain: float32 [768], replicated
- delta_second_shift: float32 [768], replicated
- delta_hidden_weight: float32 [768, 3072], P(None, 'tensor')
- delta_hidden_bias: float32 [3072], P('tensor')
- delta_return_weight: float32 [3072, 768], P('tensor')
- delta_return_bias: float32 [768], replicated
- delta_third_gain: float32 [768], replicated
- delta_third_shift: float32 [768], replicated
The draws below stay inside these ranges and needn't reach their ends.
Inputs may be any that keep to these rules, and one draw needn't show every extreme that they name: `span_counts`: valid spans of each item; some item has 4 and some has one. `retrieved`: each row of item i holds 256 distinct positions, all below span_counts[i] * 512.
All inputs are finite; a program needn't handle non-finite values.
Results may differ from the reference program's by a relative error of at most 0.025.
The reference program's roundings to bfloat16 on the way count: a program that leaves them out, or rounds other values in their place, can miss the bound.
Values may be sent and summed in bfloat16 or wider, within the bound.
A program may use at most 192 MiB of HBM per device.

```python
import jax
import jax.numpy as jnp
from jax import lax

D = 768
HEADS = 12
HD = 64
FF = 3072
L = 1024
SPAN = 512
MAXCH = 4
KR = 256
ITEMS = 8
ENC = 2048


def span_table(key):
    item_key = jax.random.fold_in(key, 7)
    counts = jax.random.randint(item_key, (ITEMS,), 1, MAXCH + 1)
    counts = counts.at[0].set(MAXCH).at[1].set(1)
    return counts.astype(jnp.int32)


def draw_span_counts(key, part):
    return span_table(key)


def draw_retrieved(key, part):
    counts = span_table(key)
    pick_key = jax.random.fold_in(key, 11)
    positions = jnp.arange(ENC, dtype=jnp.int32)
    first_row = jnp.arange(L, dtype=jnp.int32)[:, None] == 0

    def one_item(index):
        item_key = jax.random.fold_in(pick_key, index)
        raw_scores = jax.random.randint(item_key, (L, ENC), 0, 2 ** 18) * ENC + positions[None, :]
        limit = counts[index] * SPAN
        raw_scores = jnp.where(positions[None, :] < limit, raw_scores, -1)
        forced = first_row & ((positions[None, :] == 0) | (positions[None, :] == limit - 1))
        raw_scores = jnp.where(forced, 2 ** 30 + positions[None, :], raw_scores)
        return lax.top_k(raw_scores, KR)[1].astype(jnp.int32)
    return lax.map(one_item, jnp.arange(ITEMS, dtype=jnp.int32))


def levels(stream_key, dims, shards, low, top_value):
    def one(dim, shards_of):
        draws = jax.random.uniform(jax.random.fold_in(jax.random.fold_in(stream_key, 6), dim), (shards_of,), jnp.float32, low / len(shards), top_value / len(shards))
        return jnp.repeat(jnp.exp(draws), dims[dim] // shards_of).reshape((-1,) + (1,) * (len(dims) - dim - 1))

    level = one(*shards[0])
    for cut in shards[1:]:
        level = level * one(*cut)
    return level


def normal_values(rng, dims, scale, bound, cuts=(), held_as=jnp.bfloat16):
    level = levels(rng, dims, cuts, -0.22, 0.18) if cuts else 1.0
    drawn = jax.random.normal(rng, dims, jnp.float32) * scale * level
    return jnp.minimum(jnp.maximum(drawn, -bound), bound).astype(held_as)


def setup_inputs(seed: int = 0) -> dict:
    streams_of = jax.random.split(jax.random.key(seed), 30)
    decoder_input = normal_values(streams_of[0], (ITEMS, L, D), 1.0, 6.0, ((0, 8),))
    encoder_states = normal_values(streams_of[1], (ITEMS, ENC, D), 1.0, 6.0, ((0, 8),))
    span_counts = draw_span_counts(jax.random.fold_in(streams_of[29], 71), 0)
    retrieved = draw_retrieved(jax.random.fold_in(streams_of[29], 71), 0)
    self_query = normal_values(streams_of[4], (D, D), D ** -0.5, 0.21875, ((1, 4),))
    self_query_bias = normal_values(streams_of[5], (D,), 0.5, 3.0, ((0, 4),))
    self_key = normal_values(streams_of[6], (D, D), D ** -0.5, 0.21875, ((1, 4),))
    self_value = normal_values(streams_of[7], (D, D), D ** -0.5, 0.21875, ((1, 4),))
    self_value_bias = normal_values(streams_of[8], (D,), 0.5, 3.0, ((0, 4),))
    self_output = normal_values(streams_of[9], (D, D), (max(D // 256, 1)) ** -0.5, 3.5, ((0, 4),))
    self_output_bias = normal_values(streams_of[10], (D,), 0.3, 2.0)
    first_gain = jnp.clip(1.0 + 0.1 * jax.random.normal(streams_of[11], (D,), jnp.float32), 0.5, 1.5).astype(jnp.bfloat16)
    first_shift = normal_values(streams_of[12], (D,), 0.3, 2.0)
    cross_query = normal_values(streams_of[13], (D, D), D ** -0.5, 0.21875, ((1, 4),))
    cross_query_bias = normal_values(streams_of[14], (D,), 0.5, 3.0, ((0, 4),))
    cross_key = normal_values(streams_of[15], (D, D), D ** -0.5, 0.21875, ((1, 4),))
    cross_value = normal_values(streams_of[16], (D, D), D ** -0.5, 0.21875, ((1, 4),))
    cross_value_bias = normal_values(streams_of[17], (D,), 0.5, 3.0, ((0, 4),))
    cross_output = normal_values(streams_of[18], (D, D), (max(D // 256, 1)) ** -0.5, 3.5, ((0, 4),))
    cross_output_bias = normal_values(streams_of[19], (D,), 0.3, 2.0)
    second_gain = jnp.clip(1.0 + 0.1 * jax.random.normal(streams_of[20], (D,), jnp.float32), 0.5, 1.5).astype(jnp.bfloat16)
    second_shift = normal_values(streams_of[21], (D,), 0.3, 2.0)
    hidden_weight = normal_values(streams_of[22], (D, FF), D ** -0.5, 0.21875, ((1, 4),))
    hidden_bias = normal_values(streams_of[23], (FF,), 0.3, 2.0, ((0, 4),))
    return_weight = normal_values(streams_of[24], (FF, D), FF ** -0.5, 0.109375, ((0, 4),))
    return_bias = normal_values(streams_of[25], (D,), 0.3, 2.0)
    third_gain = jnp.clip(1.0 + 0.1 * jax.random.normal(streams_of[26], (D,), jnp.float32), 0.5, 1.5).astype(jnp.bfloat16)
    third_shift = normal_values(streams_of[27], (D,), 0.3, 2.0)
    cotangent = normal_values(streams_of[28], (ITEMS, L, D), 1.0, 6.0, ((0, 8),))
    return {"decoder_input": decoder_input, "encoder_states": encoder_states, "span_counts": span_counts, "retrieved": retrieved, "self_query": self_query, "self_query_bias": self_query_bias, "self_key": self_key, "self_value": self_value, "self_value_bias": self_value_bias, "self_output": self_output, "self_output_bias": self_output_bias, "first_gain": first_gain, "first_shift": first_shift, "cross_query": cross_query, "cross_query_bias": cross_query_bias, "cross_key": cross_key, "cross_value": cross_value, "cross_value_bias": cross_value_bias, "cross_output": cross_output, "cross_output_bias": cross_output_bias, "second_gain": second_gain, "second_shift": second_shift, "hidden_weight": hidden_weight, "hidden_bias": hidden_bias, "return_weight": return_weight, "return_bias": return_bias, "third_gain": third_gain, "third_shift": third_shift, "cotangent": cotangent}


@jax.custom_vjp
def low(v):
    return lax.optimization_barrier(v.astype(jnp.bfloat16)).astype(jnp.float32)

@jax.custom_vjp
def low_back(v):
    return v

def low_keep(v):
    return (low(v), None)

def low_pass(kept, grad):
    return (grad,)

def back_keep(v):
    return (v, None)

def back_low(kept, grad):
    return (low(grad),)
low.defvjp(low_keep, low_pass)
low_back.defvjp(back_keep, back_low)

def product(left, right):
    return jnp.dot(left, right, precision=lax.Precision.HIGHEST)

def layer_norm(values, gain, shift):
    mean_value = lax.optimization_barrier(jnp.mean(values, axis=-1, keepdims=True))
    centred = values - mean_value
    variance = lax.optimization_barrier(jnp.mean(centred * centred, axis=-1, keepdims=True))
    return centred * lax.rsqrt(variance + 1e-05) * gain + shift

def gelu_value(values):
    return 0.5 * values * (1.0 + lax.erf(values * 0.7071067811865476))

def split_heads(values):
    return values.reshape(values.shape[0], HEADS, HD)

def attention(queries, keys, values, allowed):
    scores = low_back(jnp.einsum('rhd,shd->hrs', queries, keys, precision=lax.Precision.HIGHEST))
    scores = jnp.where(allowed[None], scores, -1e+30)
    maxima = lax.optimization_barrier(jnp.max(scores, axis=-1, keepdims=True))
    exps = jnp.exp(scores - maxima)
    probs = exps / lax.optimization_barrier(jnp.sum(exps, axis=-1, keepdims=True))
    mixed = jnp.einsum('hrs,shd->rhd', low(probs), values, precision=lax.Precision.HIGHEST)
    return low(low_back(mixed.reshape(mixed.shape[0], HEADS * HD)))

def attend_layer(query_source, key_source, query_weight, query_bias, key_weight, value_weight, value_bias, allowed):
    queries = low((low_back(product(query_source, query_weight)) + query_bias) * 0.125)
    keys = low(low_back(product(key_source, key_weight)))
    values = low(low_back(product(key_source, value_weight)) + value_bias)
    return attention(split_heads(queries), split_heads(keys), split_heads(values), allowed)

def forward(decoder, encoder, allowed_cross, params):
    self_query, self_query_bias, self_key, self_value, self_value_bias, self_output, self_output_bias, first_gain, first_shift, cross_query, cross_query_bias, cross_key, cross_value, cross_value_bias, cross_output, cross_output_bias, second_gain, second_shift, hidden_weight, hidden_bias, return_weight, return_bias, third_gain, third_shift = params
    positions = jnp.arange(decoder.shape[0])
    causal = positions[:, None] >= positions[None, :]
    mixed_one = attend_layer(decoder, decoder, self_query, self_query_bias, self_key, self_value, self_value_bias, causal)
    branch_one = low_back(product(mixed_one, self_output)) + self_output_bias
    normed_one = layer_norm(decoder + branch_one, first_gain, first_shift)
    mixed_two = attend_layer(low(normed_one), encoder, cross_query, cross_query_bias, cross_key, cross_value, cross_value_bias, allowed_cross)
    branch_two = low_back(product(mixed_two, cross_output)) + cross_output_bias
    normed_two = layer_norm(normed_one + branch_two, second_gain, second_shift)
    pre_act = low_back(product(low(normed_two), hidden_weight)) + hidden_bias
    branch_three = low_back(product(low(gelu_value(pre_act)), return_weight)) + return_bias
    return layer_norm(normed_two + branch_three, third_gain, third_shift)

def reference(decoder_input, encoder_states, span_counts, retrieved, self_query, self_query_bias, self_key, self_value, self_value_bias, self_output, self_output_bias, first_gain, first_shift, cross_query, cross_query_bias, cross_key, cross_value, cross_value_bias, cross_output, cross_output_bias, second_gain, second_shift, hidden_weight, hidden_bias, return_weight, return_bias, third_gain, third_shift, cotangent):
    params = tuple((entry.astype(jnp.float32) for entry in (self_query, self_query_bias, self_key, self_value, self_value_bias, self_output, self_output_bias, first_gain, first_shift, cross_query, cross_query_bias, cross_key, cross_value, cross_value_bias, cross_output, cross_output_bias, second_gain, second_shift, hidden_weight, hidden_bias, return_weight, return_bias, third_gain, third_shift)))
    key_positions = jnp.arange(ENC)
    row_index = jnp.arange(L)[:, None]

    def one_item(totals, inputs):
        decoder, encoder, count, picked, upstream = inputs
        hits = jnp.zeros((L, ENC), dtype=bool).at[row_index, picked].set(True)
        allowed = hits & (key_positions < count * SPAN)[None, :]
        encoder_float = encoder.astype(jnp.float32)

        def layer_fn(decoder_float, weights):
            return forward(decoder_float, encoder_float, allowed, weights)
        output, pullback = jax.vjp(layer_fn, decoder.astype(jnp.float32), params)
        input_grad, param_grads = pullback(upstream.astype(jnp.float32))
        totals = tuple((total_item + grad_item for total_item, grad_item in zip(totals, param_grads)))
        return (totals, (output.astype(jnp.bfloat16), input_grad.astype(jnp.bfloat16)))
    zero_grads = tuple((jnp.zeros(entry.shape, jnp.float32) for entry in params))
    totals, (outputs, input_grads) = lax.scan(one_item, zero_grads, (decoder_input, encoder_states, span_counts, retrieved, cotangent))
    delta_sq, delta_sqb, delta_sk, delta_sv, delta_svb, delta_so, delta_sob, delta_fg, delta_fs, delta_cq, delta_cqb, delta_ck, delta_cv, delta_cvb, delta_co, delta_cob, delta_sg, delta_ss, delta_hw, delta_hb, delta_rw, delta_rb, delta_tg, delta_ts = totals
    return (outputs, input_grads, delta_sq, delta_sqb, delta_sk, delta_sv, delta_svb, delta_so, delta_sob, delta_fg, delta_fs, delta_cq, delta_cqb, delta_ck, delta_cv, delta_cvb, delta_co, delta_cob, delta_sg, delta_ss, delta_hw, delta_hb, delta_rw, delta_rb, delta_tg, delta_ts)
```

```python
import functools

import jax
import jax.numpy as jnp
from jax import lax
from jax.experimental import pallas as pl
from jax.experimental.pallas import tpu as pltpu
from jax.sharding import PartitionSpec as P

HD = 64
SPAN = 512
TILE = 256
WORDS = 64
BF = jnp.bfloat16
F32 = jnp.float32
VM = pl.BlockSpec(memory_space=pltpu.VMEM)
SM = pl.BlockSpec(memory_space=pltpu.SMEM)


def nn(a, b):
    return lax.dot_general(a, b, (((1,), (0,)), ((), ())), preferred_element_type=F32)


def nt(a, b):
    return lax.dot_general(a, b, (((1,), (1,)), ((), ())), preferred_element_type=F32)


def tn(a, b):
    return lax.dot_general(a, b, (((0,), (0,)), ((), ())), preferred_element_type=F32)


def sds(shape, dtype):
    return jax.ShapeDtypeStruct(shape, dtype)


def call(kernel, outs, args, flops=0, nbytes=0, scratch=(), smem=(), aliases=None, vmem=40):
    specs = [SM if i in smem else VM for i in range(len(args))]
    return pl.pallas_call(
        kernel,
        out_shape=outs,
        in_specs=specs,
        out_specs=[VM] * len(outs),
        scratch_shapes=list(scratch),
        input_output_aliases=aliases or {},
        cost_estimate=pl.CostEstimate(flops=flops, bytes_accessed=nbytes, transcendentals=0),
        compiler_params=pltpu.CompilerParams(vmem_limit_bytes=vmem << 20),
    )(*args)


def fold(x, op):
    x = x.reshape(x.shape[0] // 8, 8, x.shape[1])
    return op(x, axis=0)


def bits_kernel(limit_ref, picked_ref, out_ref, word_ref, bit_ref):
    spans = limit_ref[0]
    picked = picked_ref[...]
    word_ref[...] = picked & (WORDS - 1)
    bit_ref[...] = jnp.left_shift(jnp.ones_like(picked), jnp.right_shift(picked, 6))
    rows = picked.shape[1]
    words = lax.broadcasted_iota(jnp.int32, (WORDS, rows), 0)

    def step(i, acc):
        word = word_ref[pl.ds(i * 8, 8), :]
        bit = bit_ref[pl.ds(i * 8, 8), :]
        for j in range(8):
            acc = acc | jnp.where(word[j : j + 1] == words, bit[j : j + 1], 0)
        return acc

    acc = lax.fori_loop(0, picked.shape[0] // 8, step, jnp.zeros((WORDS, rows), jnp.int32))
    planes = spans * (SPAN // WORDS)
    one = jnp.int32(1)
    keep = jnp.where(
        planes >= 32, jnp.int32(-1), jnp.left_shift(one, jnp.minimum(planes, 31)) - one
    )
    out_ref[...] = acc & keep


def retrieval_bits(span_counts, picked):
    count, rows = picked.shape
    step = 128
    return pl.pallas_call(
        bits_kernel,
        grid=(rows // step,),
        out_shape=sds((WORDS, rows), jnp.int32),
        in_specs=[SM, pl.BlockSpec((count, step), lambda i: (0, i))],
        out_specs=pl.BlockSpec((WORDS, step), lambda i: (0, i)),
        scratch_shapes=[
            pltpu.VMEM((count, step), jnp.int32),
            pltpu.VMEM((count, step), jnp.int32),
        ],
        cost_estimate=pl.CostEstimate(flops=7 << 20, bytes_accessed=60 << 20, transcendentals=0),
    )(span_counts, picked)


def keyval_kernel(src_ref, wk_ref, wv_ref, bv_ref, k3_ref, kt_ref, v3_ref, vt_ref, wkt, wvt):
    @pl.when(pl.program_id(0) == 0)
    def _():
        wkt[...] = wk_ref[...].T
        wvt[...] = wv_ref[...].T

    src = src_ref[...]
    heads = k3_ref.shape[0]
    kt = nt(wkt[...], src)
    vt = nt(wvt[...], src) + bv_ref[...]
    kt_ref[...] = kt.astype(BF)
    vt_ref[...] = vt.astype(BF)
    for h in range(heads):
        k3_ref[h] = kt[h * HD : (h + 1) * HD].T.astype(BF)
        v3_ref[h] = vt[h * HD : (h + 1) * HD].T.astype(BF)


def key_values(src, wk, wv, bv):
    rows, width = src.shape
    cols = wk.shape[1]
    heads = cols // HD
    step = 512
    return pl.pallas_call(
        keyval_kernel,
        grid=(rows // step,),
        out_shape=[
            sds((heads, rows, HD), BF),
            sds((cols, rows), BF),
            sds((heads, rows, HD), BF),
            sds((cols, rows), BF),
        ],
        in_specs=[
            pl.BlockSpec((step, width), lambda i: (i, 0)),
            pl.BlockSpec((width, cols), lambda i: (0, 0)),
            pl.BlockSpec((width, cols), lambda i: (0, 0)),
            pl.BlockSpec((cols, 1), lambda i: (0, 0)),
        ],
        out_specs=[
            pl.BlockSpec((heads, step, HD), lambda i: (0, i, 0)),
            pl.BlockSpec((cols, step), lambda i: (0, i)),
            pl.BlockSpec((heads, step, HD), lambda i: (0, i, 0)),
            pl.BlockSpec((cols, step), lambda i: (0, i)),
        ],
        scratch_shapes=[pltpu.VMEM((cols, width), BF), pltpu.VMEM((cols, width), BF)],
        cost_estimate=pl.CostEstimate(
            flops=4 * rows * width * cols, bytes_accessed=rows * width * 4, transcendentals=0
        ),
    )(src, wk, wv, bv)


def causal_tile(core, key_tile, row_tile):
    key = ((key_tile * TILE) ^ (core * TILE)) + lax.broadcasted_iota(jnp.int32, (TILE, TILE), 0)
    row = ((row_tile * TILE) ^ (core * TILE)) + lax.broadcasted_iota(jnp.int32, (TILE, TILE), 1)
    return key <= row


def masked(scores, tile, row_tile, causal, first, core, bits_ref):
    if causal:
        if tile < first:
            return scores
        return jnp.where(causal_tile(core, tile - first, row_tile), scores, -1e30)
    lanes = slice(row_tile * TILE, (row_tile + 1) * TILE)
    planes = TILE // WORDS
    bits = bits_ref[:, lanes]
    parts = []
    for j in range(planes):
        bit = tile * planes + j
        mask = jnp.int32((1 << bit) if bit < 31 else -(1 << 31))
        hit = (bits & mask) != 0
        parts.append(jnp.where(hit, scores[j * WORDS : (j + 1) * WORDS], -1e30))
    return jnp.concatenate(parts, axis=0)


def attend_kernel(
    causal,
    core_ref,
    own_ref,
    sib_ref,
    wqt_ref,
    bq_ref,
    k3_ref,
    vt_ref,
    wo_ref,
    bits_ref,
    qt_ref,
    ot_ref,
    lse_ref,
    mine_ref,
    theirs_ref,
    score_a,
    score_b,
):
    core = core_ref[0]
    heads, keys, _ = k3_ref.shape
    first = keys // TILE - 2
    scratch = (score_a, score_b)
    turn = 0
    for row_tile, src in ((1, sib_ref), (0, own_ref)):
        lanes = slice(row_tile * TILE, (row_tile + 1) * TILE)
        qt = ((nt(wqt_ref[...], src[...]) + bq_ref[...]) * 0.125).astype(BF)
        qt_ref[:, lanes] = qt
        for h in range(heads):
            score_ref = scratch[turn % 2]
            turn += 1
            cols = slice(h * HD, (h + 1) * HD)
            query = qt[cols]
            top = jnp.full((8, TILE), -jnp.inf, F32)
            for tile in range(keys // TILE):
                span = slice(tile * TILE, (tile + 1) * TILE)
                scores = nn(k3_ref[h, span, :], query)
                scores = masked(scores, tile, row_tile, causal, first, core, bits_ref)
                score_ref[span, :] = scores
                top = jnp.maximum(top, fold(scores, jnp.max))
            top = jnp.max(top, axis=0, keepdims=True)
            total = jnp.zeros((8, TILE), F32)
            out = jnp.zeros((HD, TILE), F32)
            for tile in range(keys // TILE):
                span = slice(tile * TILE, (tile + 1) * TILE)
                probs = jnp.exp(score_ref[span, :] - top)
                total = total + fold(probs, jnp.sum)
                out = out + nn(vt_ref[cols, span], probs.astype(BF))
            total = jnp.sum(total, axis=0, keepdims=True)
            ot_ref[cols, lanes] = (out / total).astype(BF)
            lse_ref[h : h + 1, lanes] = top + jnp.log(total)
        part = tn(ot_ref[:, lanes], wo_ref[...])
        if row_tile == 0:
            mine_ref[...] = part
        else:
            theirs_ref[...] = part.astype(BF)


def attend(causal, core, own, sib, wqt, bq, k3, vt, wo, bits):
    cols, width = wqt.shape
    heads, keys, _ = k3.shape
    rows = 2 * TILE
    outs = [
        sds((cols, rows), BF),
        sds((cols, rows), BF),
        sds((8, rows), F32),
        sds((TILE, width), F32),
        sds((TILE, width), BF),
    ]
    return call(
        functools.partial(attend_kernel, causal),
        outs,
        (core, own, sib, wqt, bq, k3, vt, wo, bits),
        flops=40 * heads * rows * keys * HD,
        nbytes=4 << 20,
        scratch=[pltpu.VMEM((keys, TILE), F32), pltpu.VMEM((keys, TILE), F32)],
        smem=(0,),
    )


def attend_back_kernel(
    causal,
    carry,
    split,
    core_ref,
    gown_ref,
    gsib_ref,
    wo_ref,
    qt_ref,
    ot_ref,
    lse_ref,
    bits_ref,
    k3_ref,
    v3_ref,
    kt_ref,
    w_ref,
    *rest,
):
    if carry:
        dk_in, dv_in, rest = rest[0], rest[1], rest[2:]
    if split:
        dqt_ref, dk_ref, dv_ref, dklow_ref, dvlow_ref, bias_ref, vbias_ref = rest[:7]
        rest = rest[7:]
    else:
        dqt_ref, dk_ref, dv_ref, bias_ref = rest[:4]
        rest = rest[4:]
    mine_ref, theirs_ref, dq_ref, dot_ref = rest
    core = core_ref[0]
    heads, keys, _ = k3_ref.shape
    tiles = keys // TILE
    first = tiles - 2
    bias = None
    for row_tile, src in ((0, gown_ref), (1, gsib_ref)):
        lanes = slice(row_tile * TILE, (row_tile + 1) * TILE)
        dot_ref[:, lanes] = nt(wo_ref[...], src[...]).astype(BF)
    for h in range(heads):
        cols = slice(h * HD, (h + 1) * HD)
        both = dot_ref[cols, :].astype(F32) * ot_ref[cols, :].astype(F32)
        delta = jnp.sum(both, axis=0, keepdims=True)
        grads = [jnp.zeros((HD, TILE), F32), jnp.zeros((HD, TILE), F32)]
        for tile in range(tiles):
            span = slice(tile * TILE, (tile + 1) * TILE)
            if carry:
                dk = dk_in[cols, span]
                dv = dv_in[cols, span]
            else:
                dk = jnp.zeros((HD, TILE), F32)
                dv = jnp.zeros((HD, TILE), F32)
            for row_tile in range(2):
                lanes = slice(row_tile * TILE, (row_tile + 1) * TILE)
                query = qt_ref[cols, lanes]
                grad = dot_ref[cols, lanes]
                scores = nn(k3_ref[h, span, :], query)
                scores = masked(scores, tile, row_tile, causal, first, core, bits_ref)
                probs = jnp.exp(scores - lse_ref[h : h + 1, lanes])
                prob_grad = nn(v3_ref[h, span, :], grad)
                score_grad = (probs * (prob_grad - delta[:, lanes])).astype(BF)
                dv = dv + nt(grad, probs.astype(BF))
                dk = dk + nt(query, score_grad)
                grads[row_tile] = grads[row_tile] + nn(kt_ref[cols, span], score_grad)
            dk_ref[cols, span] = dk
            dv_ref[cols, span] = dv
        for row_tile in range(2):
            lanes = slice(row_tile * TILE, (row_tile + 1) * TILE)
            dq_ref[cols, lanes] = grads[row_tile] * 0.125
    dq = dq_ref[...]
    bias_ref[...] = jnp.sum(dq, axis=1, keepdims=True)
    dqt_ref[...] = dq.astype(BF)
    if split:
        low = slice(keys - 2 * TILE, keys)
        dv = dv_ref[:, low]
        vbias_ref[...] = jnp.sum(dv, axis=1, keepdims=True)
        dklow_ref[...] = dk_ref[:, low].astype(BF)
        dvlow_ref[...] = dv.astype(BF)
    for row_tile in range(2):
        lanes = slice(row_tile * TILE, (row_tile + 1) * TILE)
        cols = dqt_ref.shape[0]
        part = tn(dqt_ref[:, lanes], w_ref[0:cols, :])
        if split:
            part = part + tn(dklow_ref[:, lanes], w_ref[cols : 2 * cols, :])
            part = part + tn(dvlow_ref[:, lanes], w_ref[2 * cols : 3 * cols, :])
        if row_tile == 0:
            mine_ref[...] = part
        else:
            theirs_ref[...] = part.astype(BF)


def attend_back(causal, core, gown, gsib, wo, qt, ot, lse, bits, k3, v3, kt, w, carried=None):
    cols, width = wo.shape
    heads, keys, _ = k3.shape
    rows = 2 * TILE
    outs = [sds((cols, rows), BF), sds((cols, keys), F32), sds((cols, keys), F32)]
    if causal:
        outs += [sds((cols, rows), BF), sds((cols, rows), BF)]
    outs += [sds((cols, 1), F32)] * (2 if causal else 1)
    outs += [sds((TILE, width), F32), sds((TILE, width), BF)]
    args = (core, gown, gsib, wo, qt, ot, lse, bits, k3, v3, kt, w)
    if carried:
        args = args + tuple(carried)
    return call(
        functools.partial(attend_back_kernel, causal, bool(carried), causal),
        outs,
        args,
        flops=100 * heads * rows * keys * HD,
        nbytes=8 << 20,
        scratch=[pltpu.VMEM((cols, rows), F32), pltpu.VMEM((cols, rows), BF)],
        smem=(0,),
    )


def ffn_kernel(own_ref, sib_ref, w1_ref, b1_ref, w2_ref, pre_ref, act_ref, mine_ref, theirs_ref):
    for row_tile, src in ((1, sib_ref), (0, own_ref)):
        rows = slice(row_tile * TILE, (row_tile + 1) * TILE)
        pre = nn(src[...], w1_ref[...]) + b1_ref[...]
        pre_ref[rows, :] = pre
        act_ref[rows, :] = (0.5 * pre * (1.0 + lax.erf(pre * 0.7071067811865476))).astype(BF)
        part = nn(act_ref[rows, :], w2_ref[...])
        if row_tile == 0:
            mine_ref[...] = part
        else:
            theirs_ref[...] = part.astype(BF)


def ffn(own, sib, w1, b1, w2):
    width, hidden = w1.shape
    rows = 2 * TILE
    outs = [
        sds((rows, hidden), F32),
        sds((rows, hidden), BF),
        sds((TILE, width), F32),
        sds((TILE, width), BF),
    ]
    return call(ffn_kernel, outs, (own, sib, w1, b1, w2), 4 * rows * width * hidden, 6 << 20)


def ffn_back_kernel(
    own_ref, sib_ref, w2_ref, pre_ref, w1_ref, low_ref, bias_ref, mine_ref, theirs_ref
):
    bias = jnp.zeros((1, pre_ref.shape[1]), F32)
    for row_tile, src in ((1, sib_ref), (0, own_ref)):
        rows = slice(row_tile * TILE, (row_tile + 1) * TILE)
        pre = pre_ref[rows, :]
        slope = 0.5 * (1.0 + lax.erf(pre * 0.7071067811865476)) + pre * (
            0.3989422804014327 * jnp.exp(-0.5 * pre * pre)
        )
        grad = nt(src[...], w2_ref[...]) * slope
        bias = bias + jnp.sum(grad, axis=0, keepdims=True)
        low_ref[rows, :] = grad.astype(BF)
        part = nt(low_ref[rows, :], w1_ref[...])
        if row_tile == 0:
            mine_ref[...] = part
        else:
            theirs_ref[...] = part.astype(BF)
    bias_ref[...] = bias


def ffn_back(own, sib, w2, pre, w1):
    width, hidden = w1.shape
    rows = 2 * TILE
    outs = [
        sds((rows, hidden), BF),
        sds((1, hidden), F32),
        sds((TILE, width), F32),
        sds((TILE, width), BF),
    ]
    return call(ffn_back_kernel, outs, (own, sib, w2, pre, w1), 4 * rows * width * hidden, 6 << 20)


def ffn_weights_kernel(n, *refs):
    acts, lows, gown, gsib, nown, nsib = (refs[i * n : (i + 1) * n] for i in range(6))
    dw1_ref, dw2_ref = refs[6 * n :]
    dw2 = dw1 = None
    for c in range(n):
        for row_tile, (g, m) in enumerate(((gown[c], nown[c]), (gsib[c], nsib[c]))):
            rows = slice(row_tile * TILE, (row_tile + 1) * TILE)
            one = tn(acts[c][rows, :], g[...])
            two = tn(m[...], lows[c][rows, :])
            dw2 = one if dw2 is None else dw2 + one
            dw1 = two if dw1 is None else dw1 + two
    dw1_ref[...] = dw1.astype(BF)
    dw2_ref[...] = dw2.astype(BF)


def ffn_weights(acts, lows, grads, normed):
    n = len(acts)
    hidden = acts[0].shape[1]
    width = grads[0][0].shape[1]
    args = (
        list(acts)
        + list(lows)
        + [g[0] for g in grads]
        + [g[1] for g in grads]
        + [m[0] for m in normed]
        + [m[1] for m in normed]
    )
    return call(
        functools.partial(ffn_weights_kernel, n),
        [sds((width, hidden), BF), sds((hidden, width), BF)],
        args,
        8 * n * TILE * width * hidden,
        10 << 20,
    )


def attn_weights_kernel(n, *refs):
    dqt, ot, gown, gsib, nown, nsib = (refs[i * n : (i + 1) * n] for i in range(6))
    rest = refs[6 * n :]
    m = (len(rest) - 5) // 3
    dkt, dvt, src = rest[:m], rest[m : 2 * m], rest[2 * m : 3 * m]
    dwq_ref, dwk_ref, dwv_ref, dwo_ref, bias_ref = rest[3 * m :]
    dwq = dwo = dwk = dwv = bias = None
    for c in range(n):
        for row_tile, (g, s) in enumerate(((gown[c], nown[c]), (gsib[c], nsib[c]))):
            lanes = slice(row_tile * TILE, (row_tile + 1) * TILE)
            one = nn(dqt[c][:, lanes], s[...])
            two = nn(ot[c][:, lanes], g[...])
            dwq = one if dwq is None else dwq + one
            dwo = two if dwo is None else dwo + two
    for c in range(m):
        dv = dvt[c][...]
        one = nn(dkt[c][...].astype(BF), src[c][...])
        two = nn(dv.astype(BF), src[c][...])
        three = jnp.sum(dv.astype(F32), axis=1, keepdims=True)
        dwk = one if dwk is None else dwk + one
        dwv = two if dwv is None else dwv + two
        bias = three if bias is None else bias + three
    dwq_ref[...] = dwq.T.astype(BF)
    dwk_ref[...] = dwk.T.astype(BF)
    dwv_ref[...] = dwv.T.astype(BF)
    dwo_ref[...] = dwo.astype(BF)
    bias_ref[...] = bias


def attn_weights(dqt, ot, grads, normed, dkt, dvt, src):
    n = len(dqt)
    cols = dqt[0].shape[0]
    width = grads[0][0].shape[1]
    args = (
        list(dqt)
        + list(ot)
        + [g[0] for g in grads]
        + [g[1] for g in grads]
        + [m[0] for m in normed]
        + [m[1] for m in normed]
        + list(dkt)
        + list(dvt)
        + list(src)
    )
    keys = sum(s.shape[0] for s in src)
    return call(
        functools.partial(attn_weights_kernel, n),
        [sds((width, cols), BF)] * 3 + [sds((cols, width), BF), sds((cols, 1), F32)],
        args,
        4 * (keys + 2 * n * TILE) * width * cols,
        12 << 20,
    )


def normalise(total):
    mean = jnp.mean(total, axis=-1, keepdims=True)
    centred = total - mean
    variance = jnp.mean(centred * centred, axis=-1, keepdims=True)
    scale = lax.rsqrt(variance + 1e-05)
    return centred * scale, scale


def pull_norm(cot, hat, scale, gain):
    scaled = cot * gain
    mean = jnp.mean(scaled, axis=-1, keepdims=True)
    mean_hat = jnp.mean(scaled * hat, axis=-1, keepdims=True)
    return (scaled - mean - hat * mean_hat) * scale


def rows_sum(x):
    return jnp.sum(x, axis=0, keepdims=True)


def half_kernel(mine_ref, got_ref, out_ref):
    out_ref[...] = (mine_ref[...] + got_ref[...].astype(F32)).astype(BF)


def norm_kernel(
    a_ref, b_ref, res_ref, bias_ref, gain_ref, shift_ref, out_ref, low_ref, hat_ref, scale_ref
):
    total = a_ref[...].astype(F32) + b_ref[...].astype(F32)
    total = total + (res_ref[...].astype(F32) + bias_ref[...])
    hat, scale = normalise(total)
    normed = hat * gain_ref[...] + shift_ref[...]
    out_ref[...] = normed
    low_ref[...] = normed.astype(BF)
    hat_ref[...] = hat
    scale_ref[...] = scale


def top_kernel(
    a_ref, b_ref, res_ref, bias_ref, gain_ref, shift_ref, cot_ref, out_ref, grad_ref, low_ref, sums_ref
):
    total = a_ref[...].astype(F32) + b_ref[...].astype(F32)
    total = total + (res_ref[...] + bias_ref[...])
    hat, scale = normalise(total)
    out_ref[...] = (hat * gain_ref[...] + shift_ref[...]).astype(BF)
    cot = cot_ref[...].astype(F32)
    grad = pull_norm(cot, hat, scale, gain_ref[...])
    grad_ref[...] = grad
    low_ref[...] = grad.astype(BF)
    sums_ref[0:1, :] = rows_sum(cot * hat)
    sums_ref[1:2, :] = rows_sum(cot)
    sums_ref[2:3, :] = rows_sum(grad)


def pull_kernel(
    a_ref, b_ref, res_ref, hat_ref, scale_ref, gain_ref, grad_ref, low_ref, sums_ref
):
    cot = a_ref[...].astype(F32) + b_ref[...].astype(F32) + res_ref[...]
    hat = hat_ref[...]
    grad = pull_norm(cot, hat, scale_ref[...], gain_ref[...])
    grad_ref[...] = grad
    low_ref[...] = grad.astype(BF)
    sums_ref[0:1, :] = rows_sum(cot * hat)
    sums_ref[1:2, :] = rows_sum(cot)
    sums_ref[2:3, :] = rows_sum(grad)


def last_kernel(a_ref, b_ref, res_ref, out_ref):
    cot = a_ref[...].astype(F32) + b_ref[...].astype(F32) + res_ref[...]
    out_ref[...] = cot.astype(BF)


def body(group, *arrays):
    (
        decoder_input,
        encoder_states,
        span_counts,
        retrieved,
        self_query,
        self_query_bias,
        self_key,
        self_value,
        self_value_bias,
        self_output,
        self_output_bias,
        first_gain,
        first_shift,
        cross_query,
        cross_query_bias,
        cross_key,
        cross_value,
        cross_value_bias,
        cross_output,
        cross_output_bias,
        second_gain,
        second_shift,
        hidden_weight,
        hidden_bias,
        return_weight,
        return_bias,
        third_gain,
        third_shift,
        cotangent,
    ) = arrays
    rows, width = decoder_input.shape[1:]
    cols = self_query.shape[1]
    chunks = rows // (2 * TILE)
    core = lax.rem(lax.axis_index("tensor"), 2)
    core_arg = core.astype(jnp.int32).reshape(1)
    to_core = [(i, i ^ 1) for i in range(group)]
    to_chip = [(i, (i + 2) % group) for i in range(group)]

    def local(x):
        parts = x.reshape((chunks, 2) + (TILE,) + x.shape[1:])
        parts = jnp.where(core == 0, parts, jnp.flip(parts, 1))
        return parts.reshape(x.shape)

    def column(x):
        return x.astype(F32).reshape(-1, 1)

    def row(x):
        return x.astype(F32).reshape(1, -1)

    decoder = local(decoder_input[0])
    encoder = encoder_states[0]
    picked = local(retrieved[0]).T
    upstream = lax.dynamic_slice_in_dim(
        cotangent[0].reshape(chunks, 2, TILE, width), core, 1, 1
    ).reshape(chunks, TILE, width)

    def piece(x, c, half):
        start = (2 * c + half) * TILE
        return x[start : start + TILE]

    order = list(range(chunks))[::-1]
    own_x = {c: piece(decoder, c, 0) for c in order}
    sib_x = {c: piece(decoder, c, 1) for c in order}

    def reduce(mine, theirs):
        got = lax.ppermute(theirs, "tensor", to_core)
        (half,) = call(half_kernel, [sds(mine.shape, BF)], (mine, got), 1 << 18, 2 << 20)
        return half, lax.ppermute(half, "tensor", to_chip)

    def share(x):
        return lax.ppermute(x, "tensor", to_core)

    self_w = jnp.concatenate([self_query.T, self_key.T, self_value.T], axis=0)
    cross_wqt = cross_query.T
    k1, kt1, v1, vt1 = key_values(decoder, self_key, self_value, column(self_value_bias))
    k2, kt2, v2, vt2 = key_values(encoder, cross_key, cross_value, column(cross_value_bias))
    bits = retrieval_bits(span_counts, picked)
    bits_of = {c: bits[:, 2 * c * TILE : 2 * (c + 1) * TILE] for c in order}
    none = jnp.zeros((8, 128), jnp.int32)

    def norm(mine, theirs, residual, bias, gain, shift):
        a, b = reduce(mine, theirs)
        outs = [sds((TILE, width), t) for t in (F32, BF, F32)] + [sds((TILE, 1), F32)]
        return call(
            norm_kernel, outs, (a, b, residual, row(bias), row(gain), row(shift)), 1 << 22, 4 << 20
        )

    def pull(mine, theirs, residual, hat, scale, gain):
        a, b = reduce(mine, theirs)
        outs = [sds((TILE, width), F32), sds((TILE, width), BF), sds((8, width), F32)]
        return call(pull_kernel, outs, (a, b, residual, hat, scale, row(gain)), 1 << 22, 4 << 20)

    fwd1, fwd2, fwd3 = {}, {}, {}
    n1, n2, g3, g2, g1 = {}, {}, {}, {}, {}
    wqt1 = self_w[:cols]
    for c in order:
        keys = 2 * (c + 1) * TILE
        qt, ot, lse, mine, theirs = attend(
            True, core_arg, own_x[c], sib_x[c], wqt1, column(self_query_bias),
            k1[:, :keys], vt1[:, :keys], self_output, none,
        )
        fwd1[c] = (qt, ot, lse)
        normed, low, hat, scale = norm(
            mine, theirs, own_x[c], self_output_bias, first_gain, first_shift
        )
        n1[c] = (normed, hat, scale, low, share(low))
    for c in order:
        normed, _, _, low, sib = n1[c]
        qt, ot, lse, mine, theirs = attend(
            False, core_arg, low, sib, cross_wqt, column(cross_query_bias),
            k2, vt2, cross_output, bits_of[c],
        )
        fwd2[c] = (qt, ot, lse)
        normed, low, hat, scale = norm(
            mine, theirs, normed, cross_output_bias, second_gain, second_shift
        )
        n2[c] = (normed, hat, scale, low, share(low))
    outputs = {}
    sums3, sums2, sums1 = {}, {}, {}
    for c in order:
        normed, _, _, low, sib = n2[c]
        pre, act, mine, theirs = ffn(low, sib, hidden_weight, row(hidden_bias), return_weight)
        a, b = reduce(mine, theirs)
        outs = [sds((TILE, width), t) for t in (BF, F32, BF)] + [sds((8, width), F32)]
        out, grad, low, sums3[c] = call(
            top_kernel,
            outs,
            (a, b, normed, row(return_bias), row(third_gain), row(third_shift), upstream[c]),
            1 << 22,
            4 << 20,
        )
        fwd3[c] = (pre, act)
        outputs[c] = (out, share(out))
        g3[c] = (grad, low, share(low))
    lows, hidden_sums = {}, {}
    for c in order:
        grad, low, sib = g3[c]
        lows[c], hidden_sums[c], mine, theirs = ffn_back(
            low, sib, return_weight, fwd3[c][0], hidden_weight
        )
        grad, low, sums2[c] = pull(mine, theirs, grad, n2[c][1], n2[c][2], second_gain)
        g2[c] = (grad, low, share(low))
    dw1, dw2 = ffn_weights(
        [fwd3[c][1] for c in order],
        [lows[c] for c in order],
        [g3[c][1:] for c in order],
        [n2[c][3:] for c in order],
    )
    dw1, dw2 = lax.psum((dw1, dw2), "dp")
    carried = None
    dq2, dq1, qb2, qb1 = {}, {}, {}, {}
    for c in order:
        grad, low, sib = g2[c]
        dq2[c], dk, dv, qb2[c], mine, theirs = attend_back(
            False, core_arg, low, sib, cross_output, *fwd2[c], bits_of[c], k2, v2, kt2,
            cross_wqt, carried,
        )
        carried = (dk, dv)
        grad, low, sums1[c] = pull(mine, theirs, grad, n1[c][1], n1[c][2], first_gain)
        g1[c] = (grad, low, share(low))
    cross_w_grads = attn_weights(
        [dq2[c] for c in order],
        [fwd2[c][1] for c in order],
        [g2[c][1:] for c in order],
        [n1[c][3:] for c in order],
        [carried[0]],
        [carried[1]],
        [encoder],
    )
    carried = None
    deltas, dk1, dv1, vb1 = {}, {}, {}, {}
    for c in order:
        keys = 2 * (c + 1) * TILE
        grad, low, sib = g1[c]
        if carried:
            carried = tuple(x[:, :keys] for x in carried)
        dq1[c], dk, dv, dk1[c], dv1[c], qb1[c], vb1[c], mine, theirs = attend_back(
            True, core_arg, low, sib, self_output, *fwd1[c], none,
            k1[:, :keys], v1[:, :keys], kt1[:, :keys], self_w, carried,
        )
        carried = (dk, dv)
        a, b = reduce(mine, theirs)
        (out,) = call(last_kernel, [sds((TILE, width), BF)], (a, b, grad), 1 << 20, 2 << 20)
        deltas[c] = (out, share(out))
    self_w_grads = attn_weights(
        [dq1[c] for c in order],
        [fwd1[c][1] for c in order],
        [g1[c][1:] for c in order],
        [(own_x[c], sib_x[c]) for c in order],
        [dk1[c] for c in order],
        [dv1[c] for c in order],
        [decoder[2 * c * TILE : 2 * (c + 1) * TILE] for c in order],
    )

    def assemble(parts):
        whole = jnp.stack([jnp.stack(parts[c]) for c in range(chunks)])
        return jnp.where(core == 0, whole, jnp.flip(whole, 1)).reshape(1, rows, width)

    def over_chunks(sums):
        return sum(sums[c] for c in order)

    wide = jnp.concatenate(
        [over_chunks(s)[0:3] for s in (sums1, sums2, sums3)] + [jnp.zeros((7, width), F32)]
    )
    wide = wide + share(wide)
    narrow = jnp.concatenate(
        [over_chunks(qb1), over_chunks(vb1), over_chunks(qb2), cross_w_grads[4]], axis=0
    ).reshape(1, 4 * cols)
    small = jnp.concatenate([wide[0:9], jnp.zeros((7, width), F32)]).astype(BF)
    inner = jnp.concatenate(
        [narrow, over_chunks(hidden_sums), jnp.zeros((14, narrow.shape[1]), F32)]
    ).astype(BF)
    (
        (dcq, dck, dcv, dco),
        (dsq, dsk, dsv, dso),
        small,
        inner,
    ) = lax.psum((tuple(cross_w_grads[:4]), tuple(self_w_grads[:4]), small, inner), "dp")
    small = small.astype(F32)
    inner = inner.astype(F32)
    f = lambda x: x.astype(F32)
    return (
        assemble(outputs),
        assemble(deltas),
        f(dsq),
        inner[0, 0:cols],
        f(dsk),
        f(dsv),
        inner[0, cols : 2 * cols],
        f(dso),
        small[2],
        small[0],
        small[1],
        f(dcq),
        inner[0, 2 * cols : 3 * cols],
        f(dck),
        f(dcv),
        inner[0, 3 * cols : 4 * cols],
        f(dco),
        small[5],
        small[3],
        small[4],
        f(dw1),
        inner[1],
        f(dw2),
        small[8],
        small[6],
        small[7],
    )


def solution(mesh):
    acts = P("dp", None, None)
    col, vec, rowp, rep = P(None, "tensor"), P("tensor"), P("tensor", None), P()
    attn_in = (col, vec, col, col, vec, rowp, rep, rep, rep)
    placed = (acts, acts, P("dp"), acts) + attn_in + attn_in
    placed = placed + (col, vec, rowp, rep, rep, rep, acts)
    outs = (acts, acts) + attn_in + attn_in + (col, vec, rowp, rep, rep, rep)
    return jax.shard_map(
        functools.partial(body, mesh.shape["tensor"]),
        mesh=mesh,
        in_specs=placed,
        out_specs=outs,
        check_vma=False,
    )
```

```python
import functools

import jax
import jax.numpy as jnp
from jax import lax
from jax.experimental import pallas as pl
from jax.experimental.pallas import tpu as pltpu
from jax.sharding import PartitionSpec as P

HD = 64
SPAN = 512
TILE = 256
WORDS = 64
BF = jnp.bfloat16
F32 = jnp.float32
VM = pl.BlockSpec(memory_space=pltpu.VMEM)
SM = pl.BlockSpec(memory_space=pltpu.SMEM)


def nn(a, b):
    return lax.dot_general(a, b, (((1,), (0,)), ((), ())), preferred_element_type=F32)


def nt(a, b):
    return lax.dot_general(a, b, (((1,), (1,)), ((), ())), preferred_element_type=F32)


def tn(a, b):
    return lax.dot_general(a, b, (((0,), (0,)), ((), ())), preferred_element_type=F32)


def sds(shape, dtype):
    return jax.ShapeDtypeStruct(shape, dtype)


def call(kernel, outs, args, flops=0, nbytes=0, scratch=(), smem=(), aliases=None, vmem=40):
    specs = [SM if i in smem else VM for i in range(len(args))]
    return pl.pallas_call(
        kernel,
        out_shape=outs,
        in_specs=specs,
        out_specs=[VM] * len(outs),
        scratch_shapes=list(scratch),
        input_output_aliases=aliases or {},
        cost_estimate=pl.CostEstimate(flops=flops, bytes_accessed=nbytes, transcendentals=0),
        compiler_params=pltpu.CompilerParams(vmem_limit_bytes=vmem << 20),
    )(*args)


def fold(x, op):
    x = x.reshape(x.shape[0] // 8, 8, x.shape[1])
    return op(x, axis=0)


def bits_kernel(limit_ref, picked_ref, after_ref, out_ref, word_ref, bit_ref):
    spans = limit_ref[0]
    picked = picked_ref[...].T
    word_ref[...] = picked & (WORDS - 1)
    bit_ref[...] = jnp.left_shift(jnp.ones_like(picked), jnp.right_shift(picked, 6))
    rows = picked.shape[1]
    words = lax.broadcasted_iota(jnp.int32, (WORDS, rows), 0)

    def step(i, acc):
        word = word_ref[pl.ds(i * 8, 8), :]
        bit = bit_ref[pl.ds(i * 8, 8), :]
        for j in range(8):
            acc = acc | jnp.where(word[j : j + 1] == words, bit[j : j + 1], 0)
        return acc

    acc = lax.fori_loop(0, picked.shape[0] // 8, step, jnp.zeros((WORDS, rows), jnp.int32))
    planes = spans * (SPAN // WORDS)
    one = jnp.int32(1)
    keep = jnp.where(
        planes >= 32, jnp.int32(-1), jnp.left_shift(one, jnp.minimum(planes, 31)) - one
    )
    out_ref[...] = acc & keep


def retrieval_bits(span_counts, picked, after):
    rows, count = picked.shape
    step = 128
    return pl.pallas_call(
        bits_kernel,
        grid=(rows // step,),
        out_shape=sds((WORDS, rows), jnp.int32),
        in_specs=[
            SM,
            pl.BlockSpec((step, count), lambda i: (i, 0)),
            pl.BlockSpec((16, 128), lambda i: (0, 0)),
        ],
        out_specs=pl.BlockSpec((WORDS, step), lambda i: (0, i)),
        scratch_shapes=[
            pltpu.VMEM((count, step), jnp.int32),
            pltpu.VMEM((count, step), jnp.int32),
        ],
        cost_estimate=pl.CostEstimate(flops=7 << 20, bytes_accessed=30 << 20, transcendentals=0),
    )(span_counts, picked, after)


def keyval_kernel(src_ref, wkt_ref, wvt_ref, bv_ref, after_ref, k3_ref, kt_ref, v3_ref, vt_ref):
    src = src_ref[...]
    heads = k3_ref.shape[0]
    kt = nt(wkt_ref[...], src)
    vt = nt(wvt_ref[...], src) + bv_ref[...]
    kt_ref[...] = kt.astype(BF)
    vt_ref[...] = vt.astype(BF)
    for h in range(heads):
        k3_ref[h] = kt[h * HD : (h + 1) * HD].T.astype(BF)
        v3_ref[h] = vt[h * HD : (h + 1) * HD].T.astype(BF)


def key_values(src, wkt, wvt, bv, after):
    rows, width = src.shape
    cols = wkt.shape[0]
    heads = cols // HD
    step = 512
    return pl.pallas_call(
        keyval_kernel,
        grid=(rows // step,),
        out_shape=[
            sds((heads, rows, HD), BF),
            sds((cols, rows), BF),
            sds((heads, rows, HD), BF),
            sds((cols, rows), BF),
        ],
        in_specs=[
            pl.BlockSpec((step, width), lambda i: (i, 0)),
            pl.BlockSpec((cols, width), lambda i: (0, 0)),
            pl.BlockSpec((cols, width), lambda i: (0, 0)),
            pl.BlockSpec((cols, 1), lambda i: (0, 0)),
            pl.BlockSpec((16, 128), lambda i: (0, 0)),
        ],
        out_specs=[
            pl.BlockSpec((heads, step, HD), lambda i: (0, i, 0)),
            pl.BlockSpec((cols, step), lambda i: (0, i)),
            pl.BlockSpec((heads, step, HD), lambda i: (0, i, 0)),
            pl.BlockSpec((cols, step), lambda i: (0, i)),
        ],
        cost_estimate=pl.CostEstimate(
            flops=4 * rows * width * cols, bytes_accessed=rows * width * 4, transcendentals=0
        ),
    )(src, wkt, wvt, bv, after)


def causal_tile(core, key_tile, row_tile):
    key = key_tile * TILE + lax.broadcasted_iota(jnp.int32, (TILE, TILE), 0)
    row = ((row_tile * TILE) ^ (core * TILE)) + lax.broadcasted_iota(jnp.int32, (TILE, TILE), 1)
    return key <= row


def at(core, c, half):
    return pl.multiple_of(2 * c * TILE + ((half * TILE) ^ (core * TILE)), TILE)


def masked(scores, tile, row_tile, causal, first, core, bits):
    if causal:
        if tile < first:
            return scores
        return jnp.where(causal_tile(core, tile - first, row_tile), scores, -1e30)
    planes = TILE // WORDS
    parts = []
    for j in range(planes):
        bit = tile * planes + j
        mask = jnp.int32((1 << bit) if bit < 31 else -(1 << 31))
        hit = (bits & mask) != 0
        parts.append(jnp.where(hit, scores[j * WORDS : (j + 1) * WORDS], -1e30))
    return jnp.concatenate(parts, axis=0)


def attend_kernel(
    causal,
    c,
    core_ref,
    own_ref,
    sib_ref,
    wqt_ref,
    bq_ref,
    k3_ref,
    vt_ref,
    wo_ref,
    bits_ref,
    qt_ref,
    ot_ref,
    lse_ref,
    mine_ref,
    theirs_ref,
    score_a,
    score_b,
):
    core = core_ref[0]
    heads, keys, _ = k3_ref.shape
    first = keys // TILE - 2
    scratch = (score_a, score_b)
    turn = 0
    for row_tile, src in ((1, sib_ref), (0, own_ref)):
        lanes = slice(row_tile * TILE, (row_tile + 1) * TILE)
        start = at(core, c, row_tile)
        rows = src[pl.ds(start, TILE), :] if causal else src[...]
        bits = None if causal else bits_ref[:, pl.ds(start, TILE)]
        qt = ((nt(wqt_ref[...], rows) + bq_ref[...]) * 0.125).astype(BF)
        qt_ref[:, lanes] = qt
        for h in range(heads):
            score_ref = scratch[turn % 2]
            turn += 1
            cols = slice(h * HD, (h + 1) * HD)
            query = qt[cols]
            top = jnp.full((8, TILE), -jnp.inf, F32)
            for tile in range(keys // TILE):
                span = slice(tile * TILE, (tile + 1) * TILE)
                scores = nn(k3_ref[h, span, :], query)
                scores = masked(scores, tile, row_tile, causal, first, core, bits)
                score_ref[span, :] = scores
                top = jnp.maximum(top, fold(scores, jnp.max))
            top = jnp.max(top, axis=0, keepdims=True)
            total = jnp.zeros((8, TILE), F32)
            out = jnp.zeros((HD, TILE), F32)
            for tile in range(keys // TILE):
                span = slice(tile * TILE, (tile + 1) * TILE)
                probs = jnp.exp(score_ref[span, :] - top)
                total = total + fold(probs, jnp.sum)
                out = out + nn(vt_ref[cols, span], probs.astype(BF))
            total = jnp.sum(total, axis=0, keepdims=True)
            ot_ref[cols, lanes] = (out / total).astype(BF)
            lse_ref[h : h + 1, lanes] = top + jnp.log(total)
        part = tn(ot_ref[:, lanes], wo_ref[...])
        if row_tile == 0:
            mine_ref[...] = part
        else:
            theirs_ref[...] = part.astype(BF)


def attend(causal, c, core, own, sib, wqt, bq, k3, vt, wo, bits):
    cols, width = wqt.shape
    heads, keys, _ = k3.shape
    rows = 2 * TILE
    outs = [
        sds((cols, rows), BF),
        sds((cols, rows), BF),
        sds((8, rows), F32),
        sds((TILE, width), F32),
        sds((TILE, width), BF),
    ]
    return call(
        functools.partial(attend_kernel, causal, c),
        outs,
        (core, own, sib, wqt, bq, k3, vt, wo, bits),
        flops=40 * heads * rows * keys * HD,
        nbytes=4 << 20,
        scratch=[pltpu.VMEM((keys, TILE), F32), pltpu.VMEM((keys, TILE), F32)],
        smem=(0,),
    )


def as_row(x):
    column = jnp.sum(x, axis=1, keepdims=True)
    return jnp.broadcast_to(column, (x.shape[0], 128)).T[0:1]


def attend_back_kernel(
    causal,
    carry,
    split,
    c,
    core_ref,
    gown_ref,
    gsib_ref,
    wo_ref,
    qt_ref,
    ot_ref,
    lse_ref,
    bits_ref,
    k3_ref,
    v3_ref,
    kt_ref,
    w_ref,
    *rest,
):
    if split:
        wk_ref, wv_ref, rest = rest[0], rest[1], rest[2:]
    if carry:
        dk_in, dv_in, rest = rest[0], rest[1], rest[2:]
    if split:
        dqt_ref, dk_ref, dv_ref, dklow_ref, dvlow_ref, bias_ref, vbias_ref = rest[:7]
        rest = rest[7:]
    else:
        dqt_ref, dk_ref, dv_ref, bias_ref = rest[:4]
        rest = rest[4:]
    mine_ref, theirs_ref, dq_ref, dot_ref = rest
    core = core_ref[0]
    heads, keys, _ = k3_ref.shape
    tiles = keys // TILE
    first = tiles - 2
    bias = None
    for row_tile, src in ((0, gown_ref), (1, gsib_ref)):
        lanes = slice(row_tile * TILE, (row_tile + 1) * TILE)
        dot_ref[:, lanes] = nt(wo_ref[...], src[...]).astype(BF)
    for h in range(heads):
        cols = slice(h * HD, (h + 1) * HD)
        both = dot_ref[cols, :].astype(F32) * ot_ref[cols, :].astype(F32)
        delta = jnp.sum(both, axis=0, keepdims=True)
        grads = [jnp.zeros((HD, TILE), F32), jnp.zeros((HD, TILE), F32)]
        for tile in range(tiles):
            span = slice(tile * TILE, (tile + 1) * TILE)
            if carry:
                dk = dk_in[cols, span]
                dv = dv_in[cols, span]
            else:
                dk = jnp.zeros((HD, TILE), F32)
                dv = jnp.zeros((HD, TILE), F32)
            for row_tile in range(2):
                lanes = slice(row_tile * TILE, (row_tile + 1) * TILE)
                query = qt_ref[cols, lanes]
                bits = None if causal else bits_ref[:, pl.ds(at(core, c, row_tile), TILE)]
                grad = dot_ref[cols, lanes]
                scores = nn(k3_ref[h, span, :], query)
                scores = masked(scores, tile, row_tile, causal, first, core, bits)
                probs = jnp.exp(scores - lse_ref[h : h + 1, lanes])
                prob_grad = nn(v3_ref[h, span, :], grad)
                score_grad = (probs * (prob_grad - delta[:, lanes])).astype(BF)
                dv = dv + nt(grad, probs.astype(BF))
                dk = dk + nt(query, score_grad)
                grads[row_tile] = grads[row_tile] + nn(kt_ref[cols, span], score_grad)
            dk_ref[cols, span] = dk
            dv_ref[cols, span] = dv
        for row_tile in range(2):
            lanes = slice(row_tile * TILE, (row_tile + 1) * TILE)
            dq_ref[cols, lanes] = grads[row_tile] * 0.125
    dq = dq_ref[...]
    bias_ref[...] = as_row(dq)
    dqt_ref[...] = dq.astype(BF)
    if split:
        low = slice(keys - 2 * TILE, keys)
        dv = dv_ref[:, low]
        vbias_ref[...] = as_row(dv)
        dklow_ref[...] = dk_ref[:, low].astype(BF)
        dvlow_ref[...] = dv.astype(BF)
    for row_tile in range(2):
        lanes = slice(row_tile * TILE, (row_tile + 1) * TILE)
        part = tn(dqt_ref[:, lanes], w_ref[...])
        if split:
            keys_at = pl.ds(at(core, 0, row_tile), TILE)
            part = part + tn(dklow_ref[:, keys_at], wk_ref[...])
            part = part + tn(dvlow_ref[:, keys_at], wv_ref[...])
        if row_tile == 0:
            mine_ref[...] = part
        else:
            theirs_ref[...] = part.astype(BF)


def attend_back(causal, c, core, gown, gsib, wo, qt, ot, lse, bits, k3, v3, kt, w, carried=None):
    cols, width = wo.shape
    heads, keys, _ = k3.shape
    rows = 2 * TILE
    outs = [sds((cols, rows), BF), sds((cols, keys), F32), sds((cols, keys), F32)]
    if causal:
        outs += [sds((cols, rows), BF), sds((cols, rows), BF)]
    outs += [sds((1, cols), F32)] * (2 if causal else 1)
    outs += [sds((TILE, width), F32), sds((TILE, width), BF)]
    args = (core, gown, gsib, wo, qt, ot, lse, bits, k3, v3, kt) + tuple(w)
    if carried:
        args = args + tuple(carried)
    return call(
        functools.partial(attend_back_kernel, causal, bool(carried), causal, c),
        outs,
        args,
        flops=100 * heads * rows * keys * HD,
        nbytes=8 << 20,
        scratch=[pltpu.VMEM((cols, rows), F32), pltpu.VMEM((cols, rows), BF)],
        smem=(0,),
    )


def ffn_kernel(own_ref, sib_ref, w1_ref, b1_ref, w2_ref, pre_ref, act_ref, mine_ref, theirs_ref):
    for row_tile, src in ((1, sib_ref), (0, own_ref)):
        rows = slice(row_tile * TILE, (row_tile + 1) * TILE)
        pre = nn(src[...], w1_ref[...]) + b1_ref[...]
        pre_ref[rows, :] = pre
        act_ref[rows, :] = (0.5 * pre * (1.0 + lax.erf(pre * 0.7071067811865476))).astype(BF)
        part = nn(act_ref[rows, :], w2_ref[...])
        if row_tile == 0:
            mine_ref[...] = part
        else:
            theirs_ref[...] = part.astype(BF)


def ffn(own, sib, w1, b1, w2):
    width, hidden = w1.shape
    rows = 2 * TILE
    outs = [
        sds((rows, hidden), F32),
        sds((rows, hidden), BF),
        sds((TILE, width), F32),
        sds((TILE, width), BF),
    ]
    return call(ffn_kernel, outs, (own, sib, w1, b1, w2), 4 * rows * width * hidden, 6 << 20)


def ffn_back_kernel(
    own_ref, sib_ref, w2_ref, pre_ref, w1_ref, low_ref, bias_ref, mine_ref, theirs_ref
):
    bias = jnp.zeros((1, pre_ref.shape[1]), F32)
    for row_tile, src in ((1, sib_ref), (0, own_ref)):
        rows = slice(row_tile * TILE, (row_tile + 1) * TILE)
        pre = pre_ref[rows, :]
        slope = 0.5 * (1.0 + lax.erf(pre * 0.7071067811865476)) + pre * (
            0.3989422804014327 * jnp.exp(-0.5 * pre * pre)
        )
        grad = nt(src[...], w2_ref[...]) * slope
        bias = bias + jnp.sum(grad, axis=0, keepdims=True)
        low_ref[rows, :] = grad.astype(BF)
        part = nt(low_ref[rows, :], w1_ref[...])
        if row_tile == 0:
            mine_ref[...] = part
        else:
            theirs_ref[...] = part.astype(BF)
    bias_ref[...] = bias


def ffn_back(own, sib, w2, pre, w1):
    width, hidden = w1.shape
    rows = 2 * TILE
    outs = [
        sds((rows, hidden), BF),
        sds((1, hidden), F32),
        sds((TILE, width), F32),
        sds((TILE, width), BF),
    ]
    return call(ffn_back_kernel, outs, (own, sib, w2, pre, w1), 4 * rows * width * hidden, 6 << 20)


def ffn_weights_kernel(n, *refs):
    acts, lows, gown, gsib, nown, nsib = (refs[i * n : (i + 1) * n] for i in range(6))
    dw1_ref, dw2_ref = refs[6 * n :]
    dw2 = dw1 = None
    for c in range(n):
        for row_tile, (g, m) in enumerate(((gown[c], nown[c]), (gsib[c], nsib[c]))):
            rows = slice(row_tile * TILE, (row_tile + 1) * TILE)
            one = tn(acts[c][rows, :], g[...])
            two = tn(m[...], lows[c][rows, :])
            dw2 = one if dw2 is None else dw2 + one
            dw1 = two if dw1 is None else dw1 + two
    dw1_ref[...] = dw1.astype(BF)
    dw2_ref[...] = dw2.astype(BF)


def ffn_weights(acts, lows, grads, normed):
    n = len(acts)
    hidden = acts[0].shape[1]
    width = grads[0][0].shape[1]
    args = (
        list(acts)
        + list(lows)
        + [g[0] for g in grads]
        + [g[1] for g in grads]
        + [m[0] for m in normed]
        + [m[1] for m in normed]
    )
    return call(
        functools.partial(ffn_weights_kernel, n),
        [sds((width, hidden), BF), sds((hidden, width), BF)],
        args,
        8 * n * TILE * width * hidden,
        10 << 20,
    )


def attn_weights_kernel(n, order, causal, core_ref, *refs):
    core = core_ref[0]
    dqt, ot, gown, gsib = (refs[i * n : (i + 1) * n] for i in range(4))
    rest = refs[4 * n :]
    if causal:
        (src,), rest = rest[:1], rest[1:]
    else:
        nown, nsib, (src,), rest = rest[:n], rest[n : 2 * n], rest[2 * n : 2 * n + 1], rest[2 * n + 1 :]
    m = (len(rest) - 2) // 2
    dkt, dvt = rest[:m], rest[m : 2 * m]
    out_ref, bias_ref = rest[2 * m :]
    cols = dqt[0].shape[0]
    dwq = dwo = dwk = dwv = bias = None
    for i, c in enumerate(order):
        for half, g in ((0, gown[i]), (1, gsib[i])):
            lanes = slice(half * TILE, (half + 1) * TILE)
            if causal:
                rows = src[pl.ds(at(core, c, half), TILE), :]
            else:
                rows = (nsib if half else nown)[i][...]
            one = nn(dqt[i][:, lanes], rows)
            two = nn(ot[i][:, lanes], g[...])
            dwq = one if dwq is None else dwq + one
            dwo = two if dwo is None else dwo + two
    for i in range(m):
        size = dkt[i].shape[1]
        rows = src[order[i] * size : (order[i] + 1) * size, :] if m > 1 else src[...]
        dv = dvt[i][...]
        one = nn(dkt[i][...].astype(BF), rows)
        two = nn(dv.astype(BF), rows)
        three = dv.astype(F32)
        dwk = one if dwk is None else dwk + one
        dwv = two if dwv is None else dwv + two
        if not causal:
            bias = three if bias is None else bias + three
    for i, part in enumerate((dwq, dwk, dwv, dwo)):
        out_ref[i * cols : (i + 1) * cols, :] = part.astype(BF)
    if causal:
        bias_ref[...] = jnp.zeros_like(bias_ref)
    else:
        bias_ref[...] = as_row(bias)


def attn_weights(causal, order, core, dqt, ot, grads, normed, dkt, dvt, src):
    n = len(dqt)
    cols = dqt[0].shape[0]
    width = grads[0][0].shape[1]
    args = [core] + list(dqt) + list(ot) + [g[0] for g in grads] + [g[1] for g in grads]
    if not causal:
        args += [m[0] for m in normed] + [m[1] for m in normed]
    args += [src] + list(dkt) + list(dvt)
    return call(
        functools.partial(attn_weights_kernel, n, order, causal),
        [sds((4 * cols, width), BF), sds((1, cols), F32)],
        args,
        4 * (src.shape[0] + 2 * n * TILE) * width * cols,
        12 << 20,
        smem=(0,),
    )


def normalise(total):
    mean = jnp.mean(total, axis=-1, keepdims=True)
    centred = total - mean
    variance = jnp.mean(centred * centred, axis=-1, keepdims=True)
    scale = lax.rsqrt(variance + 1e-05)
    return centred * scale, scale


def pull_norm(cot, hat, scale, gain):
    scaled = cot * gain
    mean = jnp.mean(scaled, axis=-1, keepdims=True)
    mean_hat = jnp.mean(scaled * hat, axis=-1, keepdims=True)
    return (scaled - mean - hat * mean_hat) * scale


def rows_sum(x):
    return jnp.sum(x, axis=0, keepdims=True)


def half_kernel(mine_ref, got_ref, out_ref):
    out_ref[...] = (mine_ref[...] + got_ref[...].astype(F32)).astype(BF)


def norm_kernel(
    c,
    core_ref,
    a_ref,
    b_ref,
    res_ref,
    bias_ref,
    gain_ref,
    shift_ref,
    out_ref,
    low_ref,
    hat_ref,
    scale_ref,
):
    total = a_ref[...].astype(F32) + b_ref[...].astype(F32)
    if res_ref.shape[0] == TILE:
        residual = res_ref[...]
    else:
        residual = res_ref[pl.ds(at(core_ref[0], c, 0), TILE), :].astype(F32)
    total = total + (residual + bias_ref[...])
    hat, scale = normalise(total)
    normed = hat * gain_ref[...] + shift_ref[...]
    out_ref[...] = normed
    low_ref[...] = normed.astype(BF)
    hat_ref[...] = hat
    scale_ref[...] = scale


def top_kernel(
    c, core_ref, a_ref, b_ref, res_ref, bias_ref, gain_ref, shift_ref, cot_ref, out_ref, grad_ref, low_ref, sums_ref
):
    total = a_ref[...].astype(F32) + b_ref[...].astype(F32)
    total = total + (res_ref[...] + bias_ref[...])
    hat, scale = normalise(total)
    out_ref[...] = (hat * gain_ref[...] + shift_ref[...]).astype(BF)
    cot = cot_ref[pl.ds(at(core_ref[0], c, 0), TILE), :].astype(F32)
    grad = pull_norm(cot, hat, scale, gain_ref[...])
    grad_ref[...] = grad
    low_ref[...] = grad.astype(BF)
    sums_ref[0:1, :] = rows_sum(cot * hat)
    sums_ref[1:2, :] = rows_sum(cot)
    sums_ref[2:3, :] = rows_sum(grad)


def pull_kernel(
    a_ref, b_ref, res_ref, hat_ref, scale_ref, gain_ref, grad_ref, low_ref, sums_ref
):
    cot = a_ref[...].astype(F32) + b_ref[...].astype(F32) + res_ref[...]
    hat = hat_ref[...]
    grad = pull_norm(cot, hat, scale_ref[...], gain_ref[...])
    grad_ref[...] = grad
    low_ref[...] = grad.astype(BF)
    sums_ref[0:1, :] = rows_sum(cot * hat)
    sums_ref[1:2, :] = rows_sum(cot)
    sums_ref[2:3, :] = rows_sum(grad)


def last_kernel(a_ref, b_ref, res_ref, out_ref):
    cot = a_ref[...].astype(F32) + b_ref[...].astype(F32) + res_ref[...]
    out_ref[...] = cot.astype(BF)


PIECE = 32
SKEW = 1


def total_kernel(
    links, many, *refs
):
    self_ref, cross_ref = refs[:2]
    singles = refs[2 : 2 + many]
    out_ref, in_ref, near, left, right, send, acc, low, sems = refs[2 + many :]
    size = links
    node = lax.axis_index("dp") // 2
    side = lax.rem(lax.axis_index("dp"), 2)
    pairs = in_ref.shape[0] // (4 * PIECE)

    def device(at, lane):
        return {"dp": at * 2 + lane}

    def copy(src, dst, which, f, target):
        return pltpu.make_async_remote_copy(
            src_ref=src, dst_ref=dst, send_sem=sems.at[0, which, f], recv_sem=sems.at[1, which, f],
            device_id=target, device_id_type=pl.DeviceIdType.MESH,
        )

    barrier = pltpu.get_barrier_semaphore()

    def greet(target):
        pl.semaphore_signal(barrier, inc=1, device_id=target, device_id_type=pl.DeviceIdType.MESH)

    block = self_ref.shape[0]
    in_ref[0:block, :] = self_ref[...]
    in_ref[block : 2 * block, :] = cross_ref[...]
    in_ref[2 * block :, :] = jnp.zeros_like(in_ref[2 * block :, :])
    low[...] = jnp.zeros_like(low)
    gather_small(low, singles)
    in_ref[2 * block : 2 * block + SMALL, :] = low[...].astype(BF)

    greet(device(node, 1 - side))
    pl.when(node > 0)(lambda: greet(device(node - 1, side)))
    pl.when(node < size - 1)(lambda: greet(device(node + 1, side)))
    inner = (node > 0) & (node < size - 1)
    pl.semaphore_wait(barrier, jnp.where(inner, 3, 2))

    def place(t, kind, lane):
        block = (lane * pairs + t) if kind == 2 else 2 * pairs + 2 * t + kind
        return pl.ds(pl.multiple_of(block * PIECE, PIECE), PIECE)

    def root_of(kind):
        return size // 2 - 1 + kind % 2

    def near_copy(t, kind):
        f = 3 * t + kind
        src = in_ref.at[place(t, kind, 1 - side)] if kind == 2 else send.at[f]
        return copy(src, near.at[f], 0, f, device(node, 1 - side))

    def right_copy(t, kind):
        f = 3 * t + kind
        return copy(send.at[f], left.at[f], 1, f, device(node + 1, side))

    def left_copy(t, kind):
        f = 3 * t + kind
        return copy(send.at[f], right.at[f], 2, f, device(node - 1, side))

    def spread_right(t, kind):
        rows = out_ref.at[place(t, kind, side)]
        return copy(rows, rows, 3, 3 * t + kind, device(node + 1, side))

    def spread_left(t, kind):
        rows = out_ref.at[place(t, kind, side)]
        return copy(rows, rows, 4, 3 * t + kind, device(node - 1, side))

    def gather(t):
        rows = out_ref.at[place(t, 2, side)]
        return copy(rows, rows, 5, 3 * t + 2, device(node, 1 - side))

    def reduce(t, kind):
        root, f = root_of(kind), 3 * t + kind
        acc[...] = in_ref[place(t, kind, side), :].astype(F32)
        if kind == 2:
            near_copy(t, kind).wait_recv()
            acc[...] += near[f].astype(F32)

        @pl.when((node <= root) & (node > 0))
        def _():
            right_copy(t, kind).wait_recv()
            acc[...] += left[f].astype(F32)

        @pl.when((node >= root) & (node < size - 1))
        def _():
            left_copy(t, kind).wait_recv()
            acc[...] += right[f].astype(F32)

        send[f] = acc[...].astype(BF)
        pl.when(node < root)(lambda: right_copy(t, kind).start())
        pl.when(node > root)(lambda: left_copy(t, kind).start())
        if kind < 2:
            pl.when(node == root)(lambda: near_copy(t, kind).start())

    def back(t, kind):
        root, f = root_of(kind), 3 * t + kind

        @pl.when(node == root)
        def _():
            if kind == 2:
                out_ref[place(t, kind, side), :] = send[f]
            else:
                near_copy(t, kind).wait_recv()
                whole = send[f].astype(F32) + near[f].astype(F32)
                out_ref[place(t, kind, side), :] = whole.astype(BF)

        pl.when(node < root)(lambda: spread_left(t, kind).wait_recv())
        pl.when(node > root)(lambda: spread_right(t, kind).wait_recv())
        pl.when((node <= root) & (node > 0))(lambda: spread_left(t, kind).start())
        pl.when((node >= root) & (node < size - 1))(lambda: spread_right(t, kind).start())
        if kind == 2:
            gather(t).start()

    @pl.loop(0, pairs)
    def _(t):
        near_copy(t, 2).start()

    half = size // 2

    @pl.loop(0, pairs + SKEW * (2 * half + 1))
    def _(turn):
        for kind in range(3):
            root = root_of(kind)
            far = jnp.where(node < root, node, size - 1 - node)
            t = turn - SKEW * jnp.where(node == root, half, far)
            pl.when((t >= 0) & (t < pairs))(functools.partial(reduce, t, kind))
        for kind in range(3):
            root = root_of(kind)
            t = turn - SKEW * (half + 1 + jnp.abs(node - root))
            pl.when((t >= 0) & (t < pairs))(functools.partial(back, t, kind))

    @pl.loop(0, pairs)
    def _(t):
        for kind in range(3):
            root = root_of(kind)
            pl.when(node < root)(lambda: right_copy(t, kind).wait_send())
            pl.when(node > root)(lambda: left_copy(t, kind).wait_send())
            pl.when((node <= root) & (node > 0))(lambda: spread_left(t, kind).wait_send())
            pl.when((node >= root) & (node < size - 1))(lambda: spread_right(t, kind).wait_send())
            if kind == 2:
                near_copy(t, kind).wait_send()
                gather(t).wait_send()
                gather(t).wait_recv()
            else:
                pl.when(node == root)(lambda: near_copy(t, kind).wait_send())


SMALL = 16


def gather_small(low, refs):
    wide, qb1, vb1, qb2, vb2, hidden = refs[0], refs[1:3], refs[3:5], refs[5:7], refs[7], refs[8:10]
    cols = vb2.shape[1]
    low[0:9, :] = wide[0:9, :]
    low[9:10, 0:cols] = qb1[0][...] + qb1[1][...]
    low[10:11, 0:cols] = vb1[0][...] + vb1[1][...]
    low[11:12, 0:cols] = qb2[0][...] + qb2[1][...]
    low[12:13, 0:cols] = vb2[...]
    low[13:14, :] = hidden[0][...] + hidden[1][...]


def sum_over_items(dp, own, cross, smalls):
    width = own.shape[1]
    unit = 4 * PIECE
    rows = -(-(own.shape[0] + cross.shape[0] + SMALL) // unit) * unit
    count = 3 * (rows // unit)
    slots = pltpu.VMEM((count, PIECE, width), BF)
    return pl.pallas_call(
        functools.partial(total_kernel, dp // 2, len(smalls)),
        out_shape=sds((rows, width), BF),
        in_specs=[VM] * (2 + len(smalls)),
        out_specs=VM,
        scratch_shapes=[
            pltpu.VMEM((rows, width), BF),
            slots,
            slots,
            slots,
            slots,
            pltpu.VMEM((PIECE, width), F32),
            pltpu.VMEM((SMALL, width), F32),
            pltpu.SemaphoreType.DMA((2, 6, count)),
        ],
        cost_estimate=pl.CostEstimate(flops=1 << 24, bytes_accessed=200 << 20, transcendentals=0),
        compiler_params=pltpu.CompilerParams(
            collective_id=1, has_side_effects=True, vmem_limit_bytes=40 << 20
        ),
    )(own, cross, *smalls)


def assemble_kernel(order, core_ref, *refs):
    core = core_ref[0]
    out_ref = refs[-1]
    for i, c in enumerate(order):
        for half in range(2):
            out_ref[pl.ds(at(core, c, half), TILE), :] = refs[2 * i + half][...]


def body(group, items, *arrays):
    (
        decoder_input,
        encoder_states,
        span_counts,
        retrieved,
        self_query,
        self_query_bias,
        self_key,
        self_value,
        self_value_bias,
        self_output,
        self_output_bias,
        first_gain,
        first_shift,
        cross_query,
        cross_query_bias,
        cross_key,
        cross_value,
        cross_value_bias,
        cross_output,
        cross_output_bias,
        second_gain,
        second_shift,
        hidden_weight,
        hidden_bias,
        return_weight,
        return_bias,
        third_gain,
        third_shift,
        cotangent,
    ) = arrays
    rows, width = decoder_input.shape[1:]
    cols = self_query.shape[1]
    chunks = rows // (2 * TILE)
    core = lax.rem(lax.axis_index("tensor"), 2)
    core_arg = core.astype(jnp.int32).reshape(1)
    to_core = [(i, i ^ 1) for i in range(group)]
    to_chip = [(i, (i + 2) % group) for i in range(group)]

    def column(x):
        return x.astype(F32).reshape(-1, 1)

    def row(x):
        return x.astype(F32).reshape(1, -1)

    decoder = decoder_input[0]
    encoder = encoder_states[0]
    upstream = cotangent[0]
    order = list(range(chunks))[::-1]

    def reduce(mine, theirs):
        got = lax.ppermute(theirs, "tensor", to_core)
        (half,) = call(half_kernel, [sds(mine.shape, BF)], (mine, got), 1 << 18, 2 << 20)
        return half, lax.ppermute(half, "tensor", to_chip)

    def share(x):
        return lax.ppermute(x, "tensor", to_core)

    none = jnp.zeros((8, 128), jnp.int32)
    wqt1, wkt1, wvt1 = self_query.T, self_key.T, self_value.T
    wqt2, wkt2, wvt2 = cross_query.T, cross_key.T, cross_value.T
    k1, kt1, v1, vt1 = key_values(decoder, wkt1, wvt1, column(self_value_bias), decoder)

    def norm(c, mine, theirs, residual, bias, gain, shift):
        a, b = reduce(mine, theirs)
        outs = [sds((TILE, width), t) for t in (F32, BF, F32)] + [sds((TILE, 1), F32)]
        args = (core_arg, a, b, residual, row(bias), row(gain), row(shift))
        kernel = functools.partial(norm_kernel, c)
        return call(kernel, outs, args, 1 << 22, 4 << 20, smem=(0,))

    def pull(mine, theirs, residual, hat, scale, gain):
        a, b = reduce(mine, theirs)
        outs = [sds((TILE, width), F32), sds((TILE, width), BF), sds((8, width), F32)]
        return call(pull_kernel, outs, (a, b, residual, hat, scale, row(gain)), 1 << 22, 4 << 20)

    fwd1, fwd2, fwd3 = {}, {}, {}
    n1, n2, g3, g2, g1 = {}, {}, {}, {}, {}
    for c in order:
        keys = 2 * (c + 1) * TILE
        qt, ot, lse, mine, theirs = attend(
            True, c, core_arg, decoder, decoder, wqt1, column(self_query_bias),
            k1[:, :keys], vt1[:, :keys], self_output, none,
        )
        fwd1[c] = (qt, ot, lse)
        normed, low, hat, scale = norm(
            c, mine, theirs, decoder, self_output_bias, first_gain, first_shift
        )
        n1[c] = (normed, hat, scale, low, share(low))
        if c == order[-1]:
            k2, kt2, v2, vt2 = key_values(
                encoder, wkt2, wvt2, column(cross_value_bias), theirs
            )
            bits = retrieval_bits(span_counts, retrieved[0], theirs)
    for c in order:
        normed, _, _, low, sib = n1[c]
        qt, ot, lse, mine, theirs = attend(
            False, c, core_arg, low, sib, wqt2, column(cross_query_bias),
            k2, vt2, cross_output, bits,
        )
        fwd2[c] = (qt, ot, lse)
        normed, low, hat, scale = norm(
            c, mine, theirs, normed, cross_output_bias, second_gain, second_shift
        )
        n2[c] = (normed, hat, scale, low, share(low))
    outputs = {}
    sums3, sums2, sums1 = {}, {}, {}
    for c in order:
        normed, _, _, low, sib = n2[c]
        pre, act, mine, theirs = ffn(low, sib, hidden_weight, row(hidden_bias), return_weight)
        a, b = reduce(mine, theirs)
        outs = [sds((TILE, width), t) for t in (BF, F32, BF)] + [sds((8, width), F32)]
        out, grad, low, sums3[c] = call(
            functools.partial(top_kernel, c),
            outs,
            (core_arg, a, b, normed, row(return_bias), row(third_gain), row(third_shift), upstream),
            1 << 22,
            4 << 20,
            smem=(0,),
        )
        fwd3[c] = (pre, act)
        outputs[c] = (out, share(out))
        g3[c] = (grad, low, share(low))
    lows, hidden_sums = {}, {}
    for c in order:
        grad, low, sib = g3[c]
        lows[c], hidden_sums[c], mine, theirs = ffn_back(
            low, sib, return_weight, fwd3[c][0], hidden_weight
        )
        grad, low, sums2[c] = pull(mine, theirs, grad, n2[c][1], n2[c][2], second_gain)
        g2[c] = (grad, low, share(low))
    dw1, dw2 = ffn_weights(
        [fwd3[c][1] for c in order],
        [lows[c] for c in order],
        [g3[c][1:] for c in order],
        [n2[c][3:] for c in order],
    )
    dw1, dw2 = lax.psum((dw1, dw2), "dp")
    carried = None
    dq2, dq1, qb2, qb1 = {}, {}, {}, {}
    for c in order:
        grad, low, sib = g2[c]
        dq2[c], dk, dv, qb2[c], mine, theirs = attend_back(
            False, c, core_arg, low, sib, cross_output, *fwd2[c], bits, k2, v2, kt2,
            (wqt2,), carried,
        )
        carried = (dk, dv)
        grad, low, sums1[c] = pull(mine, theirs, grad, n1[c][1], n1[c][2], first_gain)
        g1[c] = (grad, low, share(low))
    cross_grads, vb2 = attn_weights(
        False,
        order,
        core_arg,
        [dq2[c] for c in order],
        [fwd2[c][1] for c in order],
        [g2[c][1:] for c in order],
        [n1[c][3:] for c in order],
        [carried[0]],
        [carried[1]],
        encoder,
    )
    carried = None
    deltas, dk1, dv1, vb1 = {}, {}, {}, {}
    for c in order:
        keys = 2 * (c + 1) * TILE
        grad, low, sib = g1[c]
        if carried:
            carried = tuple(x[:, :keys] for x in carried)
        dq1[c], dk, dv, dk1[c], dv1[c], qb1[c], vb1[c], mine, theirs = attend_back(
            True, c, core_arg, low, sib, self_output, *fwd1[c], none,
            k1[:, :keys], v1[:, :keys], kt1[:, :keys], (wqt1, wkt1, wvt1), carried,
        )
        carried = (dk, dv)
        a, b = reduce(mine, theirs)
        (out,) = call(last_kernel, [sds((TILE, width), BF)], (a, b, grad), 1 << 20, 2 << 20)
        deltas[c] = (out, share(out))
    self_grads, _ = attn_weights(
        True,
        order,
        core_arg,
        [dq1[c] for c in order],
        [fwd1[c][1] for c in order],
        [g1[c][1:] for c in order],
        None,
        [dk1[c] for c in order],
        [dv1[c] for c in order],
        decoder,
    )

    def assemble(parts):
        pieces = [x for c in order for x in parts[c]]
        kernel = functools.partial(assemble_kernel, order)
        (whole,) = call(
            kernel, [sds((rows, width), BF)], (core_arg, *pieces), 1 << 20, 3 << 20, smem=(0,)
        )
        return whole[None]

    def over_chunks(sums):
        return sum(sums[c] for c in order)

    wide = jnp.concatenate(
        [over_chunks(s)[0:3] for s in (sums1, sums2, sums3)] + [jnp.zeros((7, width), F32)]
    )
    wide = wide + share(wide)
    smalls = [wide]
    for parts in (qb1, vb1, qb2):
        smalls += [parts[c] for c in order]
    smalls += [vb2] + [hidden_sums[c] for c in order]
    total = sum_over_items(items, self_grads, cross_grads, smalls)
    total, dw1, dw2 = lax.optimization_barrier((total, dw1, dw2))

    def weights(i):
        return total[i * cols : (i + 1) * cols].astype(F32)

    small = total[8 * cols : 8 * cols + SMALL].astype(F32)
    f = lambda x: x.astype(F32)
    return (
        assemble(outputs),
        assemble(deltas),
        weights(0).T,
        small[9, 0:cols],
        weights(1).T,
        weights(2).T,
        small[10, 0:cols],
        weights(3),
        small[2],
        small[0],
        small[1],
        weights(4).T,
        small[11, 0:cols],
        weights(5).T,
        weights(6).T,
        small[12, 0:cols],
        weights(7),
        small[5],
        small[3],
        small[4],
        f(dw1),
        small[13],
        f(dw2),
        small[8],
        small[6],
        small[7],
    )


def solution(mesh):
    acts = P("dp", None, None)
    col, vec, rowp, rep = P(None, "tensor"), P("tensor"), P("tensor", None), P()
    attn_in = (col, vec, col, col, vec, rowp, rep, rep, rep)
    placed = (acts, acts, P("dp"), acts) + attn_in + attn_in
    placed = placed + (col, vec, rowp, rep, rep, rep, acts)
    outs = (acts, acts) + attn_in + attn_in + (col, vec, rowp, rep, rep, rep)
    return jax.shard_map(
        functools.partial(body, mesh.shape["tensor"], mesh.shape["dp"]),
        mesh=mesh,
        in_specs=placed,
        out_specs=outs,
        check_vma=False,
    )
```
